256 devices in a mesh: seq: 8 (over y, x_hi), exp: 32 (over z, x_lo, core).
Axes of the slice: x: 4 (x_hi: 2, x_lo: 2; x = x_hi * 2 + x_lo), y: 4, z: 8, core: 2. Of those that a mesh axis runs over, the one named last changes fastest.
Arguments:
- tokens: bfloat16 [4096, 4096], P('exp', 'seq'), may hold values from -6 to 6
- expert_ids: int32 [4096, 8], P('exp'), may hold values from 0 to 63, all different within a row; in each aligned block of 128 rows (0 to 127, 128 to 255, ...) at most 20 rows name the same one
- gate_scores: float32 [4096, 8], P('exp'), may hold values from 0.02 to 1
- gate_proj: bfloat16 [64, 1536, 4096], P('exp', None, 'seq'), may hold values from -0.09375 to 0.09375
- up_proj: bfloat16 [64, 1536, 4096], P('exp', None, 'seq'), may hold values from -0.09375 to 0.09375
- down_proj: bfloat16 [64, 1536, 4096], P('exp', None, 'seq'), may hold values from -0.15625 to 0.15625
Outputs:
- mixed: bfloat16 [4096, 4096], P('exp', 'seq')
The draws below stay inside these ranges and needn't reach their ends.
Inputs may be any that keep to these rules, and one draw needn't show every extreme that they name: `expert_ids`: within each block of 128 rows (the rows of one index of exp) no expert is named by more than 20 rows, a bound that some block reaches; every expert is named somewhere.
All inputs are finite; a program needn't handle non-finite values.
Results may differ from the reference program's by a relative error of at most 0.029.
Values may be sent and summed in bfloat16 or wider, within the bound.
A program may use at most 128 MiB of HBM per device.

```python
import math
import jax
import jax.numpy as jnp
import numpy as np
from jax import lax

D = 4096
FF = 1536
TOPK = 8
TOK_DEV = 128
EXPERTS = 64
TOKENS = 4096
CAP = 20
N_SEQ = 8
N_EXP = 32


def block_scale(stream_key, dims, split, low, top_value):
    gain = 1.0
    for dim, blocks in split:
        draws = jax.random.uniform(jax.random.fold_in(jax.random.fold_in(stream_key, 6), dim), (blocks,), jnp.float32, low / len(split), top_value / len(split))
        gain = gain * jnp.repeat(jnp.exp(draws), dims[dim] // blocks).reshape((-1,) + (1,) * (len(dims) - 1 - dim))
    return gain


def routed_block(rng, own, number, rows, count, top, most, skew):
    order = jax.random.permutation(rng, count)
    packed, common = portions_of(count, rows * top, most, skew, True), portions_of(count, rows * top, most, skew, False)
    places = jnp.arange(count)

    def named(lengths, rotation):
        used = int((lengths > 0).sum())
        fixed = max(1, used // 4)
        passed = fixed + (places - fixed + rotation * (used - fixed)) % max(1, count - fixed)
        return jnp.zeros((count,), jnp.int32).at[order[jnp.where(places < fixed, places, passed)]].set(jnp.asarray(lengths, jnp.int32))

    lengths = jnp.where(number % 4 == 0, named(packed, number // 4), named(common, number - number // 4 - 1))
    mixed = jax.random.permutation(jax.random.fold_in(own, 3), count)
    donor, sink = mixed[0:count // 2 * 2:2], mixed[1:count // 2 * 2:2]
    slack = jnp.minimum(lengths[donor] - 1, most - lengths[sink]) // 2
    slack = jnp.where((donor == order[0]) | (sink == order[0]) | (lengths[sink] == 0), 0, jnp.maximum(slack, 0))
    passed = jax.random.randint(jax.random.fold_in(own, 4), (count // 2,), 0, 1 << 20) % (slack + 1)
    lengths = lengths.at[donor].add(-passed).at[sink].add(passed)
    items = jnp.searchsorted(jnp.cumsum(lengths), jnp.arange(rows * top), side="right").astype(jnp.int32)
    listing = items.reshape(top, rows).T
    listing = listing[jax.random.permutation(jax.random.fold_in(own, 1), rows)]
    rotation = jax.random.randint(jax.random.fold_in(own, 2), (rows, 1), 0, top)
    return jnp.take_along_axis(listing, (jnp.arange(top)[None, :] + rotation) % top, axis=1)


def portions_of(number_of, total, limit, skew, full):
    weights = [(1 << 20) // math.isqrt(grade ** skew) + 1 for grade in range(1, number_of + 1)]
    largest = limit if full else min(limit, max(-(-total // number_of), total * weights[0] // sum(weights)))
    least = 1 if total - largest >= number_of - 1 else 0
    given, surplus = [largest] + [least] * (number_of - 1), total - largest - least * (number_of - 1)
    while surplus > 0:
        movable = [i for i in range(1, number_of) if given[i] < largest] or [i for i in range(1, number_of) if given[i] < limit]
        whole, left = sum([weights[i] for i in movable]), surplus
        for i in movable:
            addition = min(limit - given[i], max(1, left * weights[i] // whole), surplus)
            given[i] = given[i] + addition
            surplus = surplus - addition
    return np.array(given)


def bell_draw(rng, dims, deviation, limit, split=(), held_as=jnp.bfloat16):
    result = deviation * jax.random.normal(rng, dims, jnp.float32)
    if split:
        result = result * block_scale(rng, dims, split, -0.22, 0.18)
    return jnp.clip(result, -limit, limit).astype(held_as)


def setup_inputs(seed: int = 0) -> dict:
    streams_of = jax.random.split(jax.random.key(seed), 7)
    tokens = bell_draw(streams_of[0], (TOKENS, D), 1.0, 6.0, ((0, 32), (1, 8)))
    expert_ids_keys = jax.random.split(jax.random.fold_in(streams_of[1], 1), TOKENS // TOK_DEV)
    expert_ids_turns = jax.random.permutation(jax.random.fold_in(streams_of[1], 3), TOKENS // TOK_DEV)
    expert_ids = jax.vmap(lambda own, number: routed_block(jax.random.fold_in(streams_of[1], 2), own, number, TOK_DEV, EXPERTS, TOPK, CAP, 1))(expert_ids_keys, expert_ids_turns).reshape((TOKENS, TOPK))
    gate_scores = jnp.clip(jnp.exp(math.log(1.0) - 3.912023 * jax.random.uniform(streams_of[2], (TOKENS, TOPK), jnp.float32) ** block_scale(streams_of[2], (TOKENS, TOPK), ((0, 32),), -0.2, 0.2)), 0.02, 1.0)
    gate_proj = bell_draw(streams_of[3], (EXPERTS, FF, D), D ** -0.5, 0.09375, ((0, 32), (2, 8)))
    up_proj = bell_draw(streams_of[4], (EXPERTS, FF, D), D ** -0.5, 0.09375, ((0, 32), (2, 8)))
    down_proj = bell_draw(streams_of[5], (EXPERTS, FF, D), FF ** -0.5, 0.15625, ((0, 32), (2, 8)))
    return {"tokens": tokens, "expert_ids": expert_ids, "gate_scores": gate_scores, "gate_proj": gate_proj, "up_proj": up_proj, "down_proj": down_proj}


def slots_of(flat_ids, experts):
    onehot = (flat_ids[..., None] == jnp.arange(experts, dtype=jnp.int32)).astype(jnp.int32)
    running = jnp.cumsum(onehot, axis=-2)
    return (jnp.sum(running * onehot, axis=-1) - 1).astype(jnp.int32)


def grouped_product(rows_in, weight):
    count = rows_in.shape[0]
    left = rows_in.astype(jnp.float32).reshape(count, N_SEQ, D // N_SEQ)
    right = weight.astype(jnp.float32).reshape(FF, N_SEQ, D // N_SEQ)
    parts = jnp.einsum("rsd,fsd->srf", left, right, precision=lax.Precision.HIGHEST)
    rounded = lax.optimization_barrier(parts.astype(jnp.bfloat16))
    return jnp.sum(rounded.astype(jnp.float32), axis=0)


def reference(tokens, expert_ids, gate_scores, gate_proj, up_proj, down_proj):
    blocks = expert_ids.reshape(N_EXP, TOK_DEV * TOPK).astype(jnp.int32)
    slot = slots_of(blocks, EXPERTS)
    source = jnp.arange(N_EXP, dtype=jnp.int32)[:, None]
    row = (source * CAP + slot).astype(jnp.int32)
    tok_index = (source * TOK_DEV + jnp.arange(TOK_DEV * TOPK, dtype=jnp.int32)[None, :] // TOPK).astype(jnp.int32)
    buffer = jnp.zeros((EXPERTS, N_EXP * CAP, D), jnp.bfloat16).at[blocks, row].set(tokens[tok_index])

    def expert(operands):
        rows_in, w_gate, w_up, w_down = operands
        gate = grouped_product(rows_in, w_gate)
        up = grouped_product(rows_in, w_up)
        hidden = (jax.nn.silu(gate) * up).astype(jnp.bfloat16)
        return jnp.dot(hidden, w_down, preferred_element_type=jnp.float32).astype(jnp.bfloat16)

    outputs = lax.map(expert, (buffer, gate_proj, up_proj, down_proj))
    picked = outputs[blocks, row].astype(jnp.float32).reshape(TOKENS, TOPK, D)
    weights = gate_scores / jnp.sum(gate_scores, axis=-1, keepdims=True)
    mixed = jnp.sum(picked * weights[:, :, None], axis=1)
    return mixed.astype(jnp.bfloat16)
```

```python
import jax
import jax.numpy as jnp
from jax import lax
from jax.sharding import PartitionSpec as P

BF = jnp.bfloat16
F32 = jnp.float32


def routing(expert_ids, experts, capacity):
    tok = expert_ids.shape[0]
    named = jnp.any(expert_ids[:, None, :] == jnp.arange(experts, dtype=jnp.int32)[None, :, None], axis=-1)
    earlier = jnp.arange(tok)[:, None] > jnp.arange(tok)[None, :]
    rank = jnp.dot(earlier.astype(BF), named.astype(BF), preferred_element_type=F32)
    code = jnp.where(named, rank, -1.0).T
    return code[:, None, :] == jnp.arange(capacity, dtype=F32)[None, :, None]


def per_device(tokens, expert_ids, gate_scores, gate_proj, up_proj, down_proj):
    n_exp = lax.axis_size("exp")
    tok, narrow = tokens.shape
    topk = expert_ids.shape[1]
    exp_dev, ff, _ = gate_proj.shape
    experts = exp_dev * n_exp
    cap = tok * topk * 5 // (4 * experts)
    place = routing(expert_ids, experts, cap)
    send = jnp.dot(place.reshape(experts * cap, tok).astype(BF), tokens, preferred_element_type=F32).astype(BF)
    arrived = lax.all_to_all(
        send.reshape(n_exp, exp_dev * cap, narrow), "exp", split_axis=0, concat_axis=0, tiled=True
    )
    rows = arrived.reshape(n_exp, exp_dev, cap, narrow).transpose(1, 0, 2, 3).reshape(exp_dev, n_exp * cap, narrow)
    parts = [
        jnp.einsum("erd,efd->erf", rows, w, preferred_element_type=F32).astype(BF) for w in (gate_proj, up_proj)
    ]
    both = jnp.concatenate(parts, axis=-1)
    mine = lax.psum_scatter(both, "seq", scatter_dimension=1, tiled=True).astype(F32)
    hidden = (jax.nn.silu(mine[..., :ff]) * mine[..., ff:]).astype(BF)
    hidden = lax.all_gather(hidden, "seq", axis=1, tiled=True)
    result = jnp.einsum("erf,efd->erd", hidden, down_proj, preferred_element_type=F32).astype(BF)
    result = result.reshape(exp_dev, n_exp, cap, narrow).transpose(1, 0, 2, 3).reshape(n_exp, exp_dev * cap, narrow)
    returned = lax.all_to_all(result, "exp", split_axis=0, concat_axis=0, tiled=True).reshape(experts * cap, narrow)
    weights = gate_scores / jnp.sum(gate_scores, axis=-1, keepdims=True)
    chosen = expert_ids[:, :, None] == jnp.arange(experts, dtype=jnp.int32)
    dense = jnp.sum(jnp.where(chosen, weights[:, :, None], 0.0), axis=1)
    spread = jnp.where(place, dense.T[:, None, :], 0.0).reshape(experts * cap, tok)
    high = spread.astype(BF)
    low = (spread - high.astype(F32)).astype(BF)
    both = jnp.einsum("pst,sd->ptd", jnp.stack([high, low]), returned, preferred_element_type=F32)
    return (both[0] + both[1]).astype(BF)


def solution(mesh):
    return jax.shard_map(
        per_device,
        mesh=mesh,
        in_specs=(
            P("exp", "seq"),
            P("exp", None),
            P("exp", None),
            P("exp", None, "seq"),
            P("exp", None, "seq"),
            P("exp", None, "seq"),
        ),
        out_specs=P("exp", "seq"),
        check_vma=False,
    )
```

```python
import functools

import jax
import jax.numpy as jnp
import numpy as np
from jax import lax
from jax.experimental import pallas as pl
from jax.experimental.pallas import tpu as pltpu
from jax.sharding import PartitionSpec as P

BF = jnp.bfloat16
F32 = jnp.float32
MESH = pl.DeviceIdType.MESH
CHUNKS = 4
ORDERS = (("a", "x", "b"), ("b", "x", "a"))


def dot(a, b):
    return jnp.dot(a, b, preferred_element_type=F32)


def dot_nt(a, b):
    return lax.dot_general(a, b, (((1,), (1,)), ((), ())), preferred_element_type=F32)


def dot_tn(a, b):
    return lax.dot_general(a, b, (((0,), (0,)), ((), ())), preferred_element_type=F32)


def cube_bit(d):
    s = lax.axis_index("seq")
    y, x = s // 2, s % 2
    return {"a": ((y + 1) // 2) % 2, "b": y // 2, "x": x}[d]


def cube_peer(d):
    s = lax.axis_index("seq")
    y, x = s // 2, s % 2
    there = {"a": (y + 1 - 2 * (y % 2)) * 2 + x, "b": (3 - y) * 2 + x, "x": y * 2 + 1 - x}[d]
    return (there, lax.axis_index("exp"))


def exp_peer(dz, dl, dc):
    e = lax.axis_index("exp")
    z, l, c = e // 4, (e // 2) % 2, e % 2
    return (((z + dz + 8) % 8) * 2 + (l + dl) % 2) * 2 + (c + dc) % 2


def offset(j, m):
    return (1 - m) * (j + 1) - m * j


PLACES = tuple((m, dl, dc) for m in range(2) for dl in range(2) for dc in range(2))


def kernel(
    tok_ref, ids_ref, score_ref, place_ref, back_ref, cmat_ref, emat_ref, gate_ref, up_ref, down_ref, out_ref,
    wg, wu, wd, code, wts, qw, snd, arr, rets, retr, part, r1, r2, r3, hid,
    w_sem, d_s, d_r, t_s, t_r, c_s, c_r,
):
    seq = lax.axis_index("seq")
    experts_dev, ff, _ = wg.shape
    half = ff // 2
    loads = [pltpu.make_async_copy(a, b, w_sem.at[i]) for i, (a, b) in enumerate(((gate_ref, wg), (up_ref, wu), (down_ref, wd)))]
    for load in loads:
        load.start()

    barrier = pltpu.get_barrier_semaphore()
    for dz in range(8):
        for dl in range(2):
            for dc in range(2):
                if (dz, dl, dc) != (0, 0, 0):
                    pl.semaphore_signal(barrier, inc=1, device_id=(seq, exp_peer(dz, dl, dc)), device_id_type=MESH)
    for d in ("a", "b", "x"):
        pl.semaphore_signal(barrier, inc=1, device_id=cube_peer(d), device_id_type=MESH)

    tok = tok_ref.shape[0]
    topk = ids_ref.shape[1]
    lane = lax.broadcasted_iota(jnp.int32, (tok, 128), 1)
    row = lax.broadcasted_iota(jnp.int32, (tok, tok), 0)
    col = lax.broadcasted_iota(jnp.int32, (tok, tok), 1)
    scores = score_ref[...]
    weights = scores / jnp.sum(scores, axis=1, keepdims=True)
    named = jnp.zeros((tok, 128), F32)
    dense = jnp.zeros((tok, 128), F32)
    ids = ids_ref[...]
    for k in range(topk):
        hit = ids[:, k : k + 1] == lane
        named = named + jnp.where(hit, 1.0, 0.0)
        dense = dense + jnp.where(hit, weights[:, k : k + 1], 0.0)
    rank = dot(jnp.where(row > col, 1.0, 0.0).astype(BF), named.astype(BF))
    code[...] = jnp.where(named > 0.5, rank, -1.0).T
    wts[...] = dense.T
    t2 = jnp.concatenate([tok_ref[:, :256], tok_ref[:, 256:]], axis=0)

    pl.semaphore_wait(barrier, 34)

    def dispatch(j, i):
        m, dl, dc = PLACES[i]
        slot = j * 8 + i
        return pltpu.make_async_remote_copy(
            src_ref=snd.at[slot], dst_ref=arr.at[slot], send_sem=d_s.at[slot], recv_sem=d_r.at[slot],
            device_id=(seq, exp_peer(-offset(j, m), dl, dc)), device_id_type=MESH,
        )

    def giveback(j, i):
        m, dl, dc = PLACES[i]
        slot = j * 8 + i
        return pltpu.make_async_remote_copy(
            src_ref=rets.at[slot], dst_ref=retr.at[slot], send_sem=t_s.at[slot], recv_sem=t_r.at[slot],
            device_id=(seq, exp_peer(offset(j, m), dl, dc)), device_id_type=MESH,
        )

    def is_self(j, i):
        return j == 0 and PLACES[i] == (1, 0, 0)

    emat = emat_ref[...] > 0.5
    cmat = cmat_ref[...]
    for j in range(CHUNKS):
        for i, (m, dl, dc) in enumerate(PLACES):
            slot = j * 8 + i
            d = exp_peer(-offset(j, m), dl, dc)
            c0, c1, w0, w1 = (ref[pl.ds(2 * d + n, 1), :] for ref in (code, wts) for n in range(2))
            c0, c1, w0, w1 = (jnp.concatenate([v, v], axis=1) for v in (c0, c1, w0, w1))
            match = jnp.where(emat, c0, c1) == cmat
            snd[slot] = dot(jnp.where(match, 1.0, 0.0).astype(BF), t2).astype(BF)
            if is_self(j, i):
                pltpu.make_async_copy(snd.at[slot], arr.at[slot], d_r.at[slot]).start()
            else:
                dispatch(j, i).start()
            qw[slot] = jnp.where(match, jnp.where(emat, w0, w1), 0.0).astype(BF)

    for load in loads:
        load.wait()

    bits = [[cube_bit(d) for d in order] for order in ORDERS]

    def exchange(j, h, step):
        b1, b2, b3 = bits[h]
        if step < 3:
            first, count, dst = (
                (4 * (1 - b1), 4, r1.at[j, h]),
                (4 * b1 + 2 * (1 - b2), 2, r2.at[j, h]),
                (4 * b1 + 2 * b2 + 1 - b3, 1, r3.at[j, h]),
            )[step]
            src = part.at[j, h, pl.ds(first, count)]
            to = ORDERS[h][step]
        else:
            first, count = ((4 * b1 + 2 * b2 + b3, 1), (4 * b1 + 2 * b2, 2), (4 * b1, 4))[step - 3]
            src = dst = hid.at[j, h, pl.ds(first, count)]
            to = ORDERS[h][5 - step]
        return pltpu.make_async_remote_copy(
            src_ref=src, dst_ref=dst, send_sem=c_s.at[j, h, step], recv_sem=c_r.at[j, h, step],
            device_id=cube_peer(to), device_id_type=MESH,
        )

    def arrival(j, h, step):
        b1, b2, b3 = bits[h]
        if step < 3:
            dst = (r1.at[j, h], r2.at[j, h], r3.at[j, h])[step]
        else:
            first, count = ((4 * b1 + 2 * b2 + 1 - b3, 1), (4 * b1 + 2 * (1 - b2), 2), (4 * (1 - b1), 4))[step - 3]
            dst = hid.at[j, h, pl.ds(first, count)]
        return pltpu.make_async_copy(dst, dst, c_r.at[j, h, step])

    def products(j):
        for i in range(8):
            slot = j * 8 + i
            pltpu.make_async_copy(arr.at[slot], arr.at[slot], d_r.at[slot]).wait()
        rows = dot(place_ref[...], arr[pl.ds(j * 8, 8)].reshape(640, 256)).astype(BF)
        for h in range(2):
            for e in range(experts_dev):
                left, right = rows[160 * e : 160 * e + 160], rows[320 + 160 * e : 480 + 160 * e]
                g, u = (
                    dot_nt(left, w[e, pl.ds(half * h, half), :256]) + dot_nt(right, w[e, pl.ds(half * h, half), 256:])
                    for w in (wg, wu)
                )
                for i in range(4):
                    part[j, h, 4 * e + i] = jnp.concatenate(
                        [g[40 * i : 40 * i + 40], u[40 * i : 40 * i + 40]], axis=0
                    ).astype(BF)
            exchange(j, h, 0).start()

    def sum1(j):
        for h in range(2):
            b1, b2, b3 = bits[h]
            arrival(j, h, 0).wait()
            for k in range(2):
                rel = 2 * (1 - b2) + k
                part[j, h, 4 * b1 + rel] = (part[j, h, 4 * b1 + rel].astype(F32) + r1[j, h, rel].astype(F32)).astype(BF)
            exchange(j, h, 1).start()

    def sum2(j):
        for h in range(2):
            b1, b2, b3 = bits[h]
            arrival(j, h, 1).wait()
            rel = 2 * b2 + 1 - b3
            part[j, h, 4 * b1 + rel] = (
                part[j, h, 4 * b1 + rel].astype(F32) + r1[j, h, rel].astype(F32) + r2[j, h, 1 - b3].astype(F32)
            ).astype(BF)
            exchange(j, h, 2).start()

    def activate(j):
        for h in range(2):
            b1, b2, b3 = bits[h]
            arrival(j, h, 2).wait()
            rel = 2 * b2 + b3
            total = (
                part[j, h, 4 * b1 + rel].astype(F32) + r1[j, h, rel].astype(F32)
                + r2[j, h, b3].astype(F32) + r3[j, h, 0].astype(F32)
            )
            g, u = total[:40], total[40:]
            v = g / (1.0 + jnp.exp(-g)) * u
            hid[j, h, 4 * b1 + rel] = jnp.concatenate([v[:, :384], v[:, 384:]], axis=0).astype(BF)
            exchange(j, h, 3).start()

    def gather(j, step):
        for h in range(2):
            arrival(j, h, step).wait()
            exchange(j, h, step + 1).start()

    def outputs(j):
        for h in range(2):
            arrival(j, h, 5).wait()
        outs = []
        for e in range(experts_dev):
            acc = jnp.zeros((160, 512), F32)
            for h in range(2):
                pieces = [hid[j, h, 4 * e + i].astype(F32) for i in range(4)]
                block = jnp.concatenate([jnp.concatenate([v[:40], v[40:]], axis=1) for v in pieces], axis=0)
                acc = acc + dot(block.astype(BF), wd[e, pl.ds(half * h, half), :])
            outs.append(acc)
        tall = jnp.concatenate([o[:, n * 256 : n * 256 + 256] for n in range(2) for o in outs], axis=0).astype(BF)
        rets[pl.ds(j * 8, 8)] = dot(back_ref[...], tall).astype(BF).reshape(8, 80, 256)
        for i in range(8):
            slot = j * 8 + i
            if is_self(j, i):
                pltpu.make_async_copy(rets.at[slot], retr.at[slot], t_r.at[slot]).start()
            else:
                giveback(j, i).start()

    stages = (
        products, sum1, sum2, activate, functools.partial(gather, step=3), functools.partial(gather, step=4), outputs,
    )
    for t in range(CHUNKS + len(stages) - 1):
        for n in (0, 6, 5, 4, 3, 2, 1):
            if 0 <= t - n < CHUNKS:
                stages[n](t - n)

    total = jnp.zeros((256, 256), F32)
    for j in range(CHUNKS):
        for i in range(8):
            slot = j * 8 + i
            pltpu.make_async_copy(retr.at[slot], retr.at[slot], t_r.at[slot]).wait()
        total = total + dot_tn(qw[pl.ds(j * 8, 8)].reshape(640, 256), retr[pl.ds(j * 8, 8)].reshape(640, 256))
    out_ref[:, :256] = total[:tok].astype(BF)
    out_ref[:, 256:] = total[tok:].astype(BF)

    for j in range(CHUNKS):
        for i in range(8):
            if not is_self(j, i):
                dispatch(j, i).wait_send()
                giveback(j, i).wait_send()
        for h in range(2):
            for step in range(6):
                exchange(j, h, step).wait_send()


def placing(cap, blocks=8):
    n = 2 * 2 * blocks * cap
    out = np.zeros((n, n), np.float32)
    for b in range(blocks):
        for f in range(2):
            for e in range(2):
                for c in range(cap):
                    out[((f * 2 + e) * blocks + b) * cap + c, ((b * 2 + f) * 2 + e) * cap + c] = 1.0
    return out


def per_device(tokens, expert_ids, gate_scores, gate_proj, up_proj, down_proj):
    cap = 20
    place = placing(cap)
    r = np.arange(4 * cap)[:, None]
    t = np.arange(256)[None, :]
    cmat = np.where(r // (2 * cap) == t // 128, r % cap, -9).astype(np.float32)
    emat = np.broadcast_to((r // cap) % 2 == 0, cmat.shape).astype(np.float32)
    vmem = pl.BlockSpec(memory_space=pltpu.VMEM)
    hbm = pl.BlockSpec(memory_space=pl.ANY)
    dma = pltpu.SemaphoreType.DMA
    weights = pltpu.VMEM(gate_proj.shape, BF)
    slabs = pltpu.VMEM((32, 80, 256), BF)
    return pl.pallas_call(
        kernel,
        out_shape=jax.ShapeDtypeStruct(tokens.shape, BF),
        in_specs=[vmem] * 7 + [hbm] * 3,
        out_specs=vmem,
        scratch_shapes=[
            weights, weights, weights,
            pltpu.VMEM((128, 128), F32), pltpu.VMEM((128, 128), F32),
            slabs, slabs, slabs, slabs, slabs,
            pltpu.VMEM((CHUNKS, 2, 8, 80, 768), BF),
            pltpu.VMEM((CHUNKS, 2, 4, 80, 768), BF),
            pltpu.VMEM((CHUNKS, 2, 2, 80, 768), BF),
            pltpu.VMEM((CHUNKS, 2, 1, 80, 768), BF),
            pltpu.VMEM((CHUNKS, 2, 8, 80, 384), BF),
            dma((3,)), dma((32,)), dma((32,)), dma((32,)), dma((32,)), dma((CHUNKS, 2, 6)), dma((CHUNKS, 2, 6)),
        ],
        compiler_params=pltpu.CompilerParams(
            collective_id=0, has_side_effects=True, vmem_limit_bytes=60 * 2**20
        ),
        name="experts",
    )(
        tokens, expert_ids, gate_scores, jnp.asarray(place, BF), jnp.asarray(place.T, BF),
        jnp.asarray(cmat), jnp.asarray(emat), gate_proj, up_proj, down_proj,
    )


def solution(mesh):
    return jax.shard_map(
        per_device,
        mesh=mesh,
        in_specs=(
            P("exp", "seq"),
            P("exp", None),
            P("exp", None),
            P("exp", None, "seq"),
            P("exp", None, "seq"),
            P("exp", None, "seq"),
        ),
        out_specs=P("exp", "seq"),
        check_vma=False,
    )
```

```python
import functools

import jax
import jax.numpy as jnp
import numpy as np
from jax import lax
from jax.experimental import pallas as pl
from jax.experimental.pallas import tpu as pltpu
from jax.sharding import PartitionSpec as P

BF = jnp.bfloat16
F32 = jnp.float32
MESH = pl.DeviceIdType.MESH
CHUNKS = 4
ORDERS = (("axb", "bxa"),) * 3 + (("abx", "bax"),)
OFFSETS = ((1, -1), (2, -2), (3, -3), (0, 4))


def dot(a, b):
    return jnp.dot(a, b, preferred_element_type=F32)


def dot_nt(a, b):
    return lax.dot_general(a, b, (((1,), (1,)), ((), ())), preferred_element_type=F32)


def dot_tn(a, b):
    return lax.dot_general(a, b, (((0,), (0,)), ((), ())), preferred_element_type=F32)


def cube_bit(d):
    s = lax.axis_index("seq")
    y, x = s // 2, s % 2
    return {"a": ((y + 1) // 2) % 2, "b": y // 2, "x": x}[d]


def cube_peer(d):
    s = lax.axis_index("seq")
    y, x = s // 2, s % 2
    there = {"a": (y + 1 - 2 * (y % 2)) * 2 + x, "b": (3 - y) * 2 + x, "x": y * 2 + 1 - x}[d]
    return (there, lax.axis_index("exp"))


def exp_peer(dz, dl, dc):
    e = lax.axis_index("exp")
    z, l, c = e // 4, (e // 2) % 2, e % 2
    return (((z + dz + 8) % 8) * 2 + (l + dl) % 2) * 2 + (c + dc) % 2


PLACES = tuple((m, dl, dc) for m in range(2) for dl in range(2) for dc in range(2))


def kernel(
    tok_ref, ids_ref, score_ref, place_ref, back_ref, cmat_ref, emat_ref, gate_ref, up_ref, down_ref, out_ref,
    wg, wu, wd, code, wts, qw, snd, arr, rets, retr, part, r1, r2, r3, hid,
    w_sem, d_s, d_r, t_s, t_r, c_s, c_r,
):
    seq = lax.axis_index("seq")
    experts_dev, ff, _ = wg.shape
    half = ff // 2
    loads = [pltpu.make_async_copy(a, b, w_sem.at[i]) for i, (a, b) in enumerate(((gate_ref, wg), (up_ref, wu), (down_ref, wd)))]
    for load in loads:
        load.start()

    barrier = pltpu.get_barrier_semaphore()
    for dz in range(8):
        for dl in range(2):
            for dc in range(2):
                if (dz, dl, dc) != (0, 0, 0):
                    pl.semaphore_signal(barrier, inc=1, device_id=(seq, exp_peer(dz, dl, dc)), device_id_type=MESH)
    for d in ("a", "b", "x"):
        pl.semaphore_signal(barrier, inc=1, device_id=cube_peer(d), device_id_type=MESH)

    topk, tok = ids_ref.shape
    expert = lax.broadcasted_iota(jnp.int32, code.shape, 0)
    row = lax.broadcasted_iota(jnp.int32, (tok, tok), 0)
    col = lax.broadcasted_iota(jnp.int32, (tok, tok), 1)
    scores = score_ref[...]
    weights = scores / jnp.sum(scores, axis=0, keepdims=True)
    named = jnp.zeros(code.shape, F32)
    dense = jnp.zeros(code.shape, F32)
    ids = ids_ref[...]
    for k in range(topk):
        hit = ids[k : k + 1] == expert
        named = named + jnp.where(hit, 1.0, 0.0)
        dense = dense + jnp.where(hit, weights[k : k + 1], 0.0)
    rank = dot(named.astype(BF), jnp.where(row < col, 1.0, 0.0).astype(BF))
    code[...] = jnp.where(named > 0.5, rank, -1.0)
    wts[...] = dense
    t2 = jnp.concatenate([tok_ref[:, :256], tok_ref[:, 256:]], axis=0)

    pl.semaphore_wait(barrier, 34)

    def dispatch(j, i):
        m, dl, dc = PLACES[i]
        slot = j * 8 + i
        return pltpu.make_async_remote_copy(
            src_ref=snd.at[slot], dst_ref=arr.at[slot], send_sem=d_s.at[slot], recv_sem=d_r.at[slot],
            device_id=(seq, exp_peer(-OFFSETS[j][m], dl, dc)), device_id_type=MESH,
        )

    def giveback(j, i):
        m, dl, dc = PLACES[i]
        slot = j * 8 + i
        return pltpu.make_async_remote_copy(
            src_ref=rets.at[slot], dst_ref=retr.at[slot], send_sem=t_s.at[slot], recv_sem=t_r.at[slot],
            device_id=(seq, exp_peer(OFFSETS[j][m], dl, dc)), device_id_type=MESH,
        )

    def is_self(j, i):
        return (OFFSETS[j][PLACES[i][0]], *PLACES[i][1:]) == (0, 0, 0)

    emat = emat_ref[...] > 0.5
    cmat = cmat_ref[...]
    for j in range(CHUNKS):
        for i, (m, dl, dc) in enumerate(PLACES):
            slot = j * 8 + i
            d = exp_peer(-OFFSETS[j][m], dl, dc)
            c0, c1, w0, w1 = (ref[pl.ds(2 * d + n, 1), :] for ref in (code, wts) for n in range(2))
            c0, c1, w0, w1 = (jnp.concatenate([v, v], axis=1) for v in (c0, c1, w0, w1))
            match = jnp.where(emat, c0, c1) == cmat
            snd[slot] = dot(jnp.where(match, 1.0, 0.0).astype(BF), t2).astype(BF)
            if is_self(j, i):
                pltpu.make_async_copy(snd.at[slot], arr.at[slot], d_r.at[slot]).start()
            else:
                dispatch(j, i).start()
            qw[slot] = jnp.where(match, jnp.where(emat, w0, w1), 0.0).astype(BF)

    for load in loads:
        load.wait()

    def copies(j, h):
        b1, b2, b3 = (cube_bit(d) for d in ORDERS[j][h])
        n1, n2, n3 = 1 - b1, 1 - b2, 1 - b3

        def at(p, q, r):
            return 4 * p + 2 * q + r

        own, third, second, last = at(b1, b2, b3), at(b1, b2, n3), at(b1, n2, b3), at(b1, n2, n3)
        return (
            (part, at(n1, n2, 0), 2, r1, 2 * n2, 0, 2 * n2),
            (part, at(n1, b2, 0), 2, r1, 2 * b2, 0, 2 * b2),
            (part, last, 1, r2, n3, 1, n3),
            (part, second, 1, r2, b3, 1, b3),
            (part, third, 1, r3, 0, 2, 0),
            (hid, own, 1, hid, own, 2, third),
            (hid, own, 1, hid, own, 1, second),
            (hid, third, 1, hid, third, 1, last),
            (hid, own, 1, hid, own, 0, at(n1, b2, b3)),
            (hid, third, 1, hid, third, 0, at(n1, b2, n3)),
            (hid, second, 1, hid, second, 0, at(n1, n2, b3)),
            (hid, last, 1, hid, last, 0, at(n1, n2, n3)),
        )

    def exchange(j, h, n):
        src, first, count, dst, there, along, _ = copies(j, h)[n]
        return pltpu.make_async_remote_copy(
            src_ref=src.at[j, h, pl.ds(first, count)], dst_ref=dst.at[j, h, pl.ds(there, count)],
            send_sem=c_s.at[j, h, n], recv_sem=c_r.at[j, h, n],
            device_id=cube_peer(ORDERS[j][h][along]), device_id_type=MESH,
        )

    def arrival(j, h, n):
        _, _, count, dst, _, _, first = copies(j, h)[n]
        ref = dst.at[j, h, pl.ds(first, count)]
        return pltpu.make_async_copy(ref, ref, c_r.at[j, h, n])

    def bits(j, h):
        return [cube_bit(d) for d in ORDERS[j][h]]

    def products(j):
        for i in range(8):
            slot = j * 8 + i
            pltpu.make_async_copy(arr.at[slot], arr.at[slot], d_r.at[slot]).wait()
        rows = dot(place_ref[...], arr[pl.ds(j * 8, 8)].reshape(640, 256)).astype(BF)
        for h in range(2):
            for e in range(experts_dev):
                left, right = rows[160 * e : 160 * e + 160], rows[320 + 160 * e : 480 + 160 * e]
                g, u = (
                    dot_nt(left, w[e, pl.ds(half * h, half), :256]) + dot_nt(right, w[e, pl.ds(half * h, half), 256:])
                    for w in (wg, wu)
                )
                for i in range(4):
                    part[j, h, 4 * e + i] = jnp.concatenate(
                        [g[40 * i : 40 * i + 40], u[40 * i : 40 * i + 40]], axis=0
                    ).astype(BF)
            exchange(j, h, 0).start()
            exchange(j, h, 1).start()

    def sum1(j):
        for h in range(2):
            b1, b2, b3 = bits(j, h)
            arrival(j, h, 0).wait()
            for n, r in ((2, 1 - b3), (3, b3)):
                rel = 2 * (1 - b2) + r
                p = 4 * b1 + rel
                part[j, h, p] = (part[j, h, p].astype(F32) + r1[j, h, rel].astype(F32)).astype(BF)
                exchange(j, h, n).start()

    def sum2(j):
        for h in range(2):
            b1, b2, b3 = bits(j, h)
            arrival(j, h, 1).wait()
            arrival(j, h, 2).wait()
            rel = 2 * b2 + 1 - b3
            p = 4 * b1 + rel
            part[j, h, p] = (
                part[j, h, p].astype(F32) + r1[j, h, rel].astype(F32) + r2[j, h, 1 - b3].astype(F32)
            ).astype(BF)
            exchange(j, h, 4).start()

    def activate(j):
        for h in range(2):
            b1, b2, b3 = bits(j, h)
            arrival(j, h, 3).wait()
            arrival(j, h, 4).wait()
            rel = 2 * b2 + b3
            p = 4 * b1 + rel
            total = (
                part[j, h, p].astype(F32) + r1[j, h, rel].astype(F32)
                + r2[j, h, b3].astype(F32) + r3[j, h, 0].astype(F32)
            )
            g, u = total[:40], total[40:]
            v = g / (1.0 + jnp.exp(-g)) * u
            hid[j, h, p] = jnp.concatenate([v[:, :384], v[:, 384:]], axis=0).astype(BF)
            for n in (5, 6, 8):
                exchange(j, h, n).start()

    def pass_on(j, pairs):
        for n, after in pairs:
            for h in range(2):
                arrival(j, h, n).wait()
                for m in after:
                    exchange(j, h, m).start()

    def outputs(j):
        for h in range(2):
            for n in (8, 9, 10, 11):
                arrival(j, h, n).wait()
        outs = []
        for e in range(experts_dev):
            acc = jnp.zeros((160, 512), F32)
            for h in range(2):
                pieces = [hid[j, h, 4 * e + i].astype(F32) for i in range(4)]
                block = jnp.concatenate([jnp.concatenate([v[:40], v[40:]], axis=1) for v in pieces], axis=0)
                acc = acc + dot(block.astype(BF), wd[e, pl.ds(half * h, half), :])
            outs.append(acc)
        tall = jnp.concatenate([o[:, n * 256 : n * 256 + 256] for n in range(2) for o in outs], axis=0).astype(BF)
        rets[pl.ds(j * 8, 8)] = dot(back_ref[...], tall).astype(BF).reshape(8, 80, 256)
        for i in range(8):
            slot = j * 8 + i
            if is_self(j, i):
                pltpu.make_async_copy(rets.at[slot], retr.at[slot], t_r.at[slot]).start()
            else:
                giveback(j, i).start()

    stages = (
        products,
        sum1,
        sum2,
        activate,
        functools.partial(pass_on, pairs=((5, (7, 9)),)),
        functools.partial(pass_on, pairs=((6, (10,)), (7, (11,)))),
        outputs,
    )
    for t in range(CHUNKS + len(stages) - 1):
        for n in (0, 6, 5, 4, 3, 2, 1):
            if 0 <= t - n < CHUNKS:
                stages[n](t - n)

    total = jnp.zeros((256, 256), F32)
    for j in range(CHUNKS):
        for i in range(8):
            slot = j * 8 + i
            pltpu.make_async_copy(retr.at[slot], retr.at[slot], t_r.at[slot]).wait()
        total = total + dot_tn(qw[pl.ds(j * 8, 8)].reshape(640, 256), retr[pl.ds(j * 8, 8)].reshape(640, 256))
    out_ref[:, :256] = total[:tok].astype(BF)
    out_ref[:, 256:] = total[tok:].astype(BF)

    for j in range(CHUNKS):
        for i in range(8):
            if not is_self(j, i):
                dispatch(j, i).wait_send()
                giveback(j, i).wait_send()
        for h in range(2):
            for n in range(12):
                exchange(j, h, n).wait_send()


def placing(cap, blocks=8):
    n = 2 * 2 * blocks * cap
    out = np.zeros((n, n), np.float32)
    for b in range(blocks):
        for f in range(2):
            for e in range(2):
                for c in range(cap):
                    out[((f * 2 + e) * blocks + b) * cap + c, ((b * 2 + f) * 2 + e) * cap + c] = 1.0
    return out


def per_device(tokens, expert_ids, gate_scores, gate_proj, up_proj, down_proj):
    cap = 20
    place = placing(cap)
    r = np.arange(4 * cap)[:, None]
    t = np.arange(256)[None, :]
    cmat = np.where(r // (2 * cap) == t // 128, r % cap, -9).astype(np.float32)
    emat = np.broadcast_to((r // cap) % 2 == 0, cmat.shape).astype(np.float32)
    vmem = pl.BlockSpec(memory_space=pltpu.VMEM)
    hbm = pl.BlockSpec(memory_space=pl.ANY)
    dma = pltpu.SemaphoreType.DMA
    weights = pltpu.VMEM(gate_proj.shape, BF)
    slabs = pltpu.VMEM((32, 80, 256), BF)
    return pl.pallas_call(
        kernel,
        out_shape=jax.ShapeDtypeStruct(tokens.shape, BF),
        in_specs=[vmem] * 7 + [hbm] * 3,
        out_specs=vmem,
        scratch_shapes=[
            weights, weights, weights,
            pltpu.VMEM((64, 128), F32), pltpu.VMEM((64, 128), F32),
            slabs, slabs, slabs, slabs, slabs,
            pltpu.VMEM((CHUNKS, 2, 8, 80, 768), BF),
            pltpu.VMEM((CHUNKS, 2, 4, 80, 768), BF),
            pltpu.VMEM((CHUNKS, 2, 2, 80, 768), BF),
            pltpu.VMEM((CHUNKS, 2, 1, 80, 768), BF),
            pltpu.VMEM((CHUNKS, 2, 8, 80, 384), BF),
            dma((3,)), dma((32,)), dma((32,)), dma((32,)), dma((32,)), dma((CHUNKS, 2, 12)), dma((CHUNKS, 2, 12)),
        ],
        compiler_params=pltpu.CompilerParams(
            collective_id=0, has_side_effects=True, vmem_limit_bytes=60 * 2**20
        ),
        name="experts",
    )(
        tokens, expert_ids.T, gate_scores.T, jnp.asarray(place, BF), jnp.asarray(place.T, BF),
        jnp.asarray(cmat), jnp.asarray(emat), gate_proj, up_proj, down_proj,
    )


def solution(mesh):
    return jax.shard_map(
        per_device,
        mesh=mesh,
        in_specs=(
            P("exp", "seq"),
            P("exp", None),
            P("exp", None),
            P("exp", None, "seq"),
            P("exp", None, "seq"),
            P("exp", None, "seq"),
        ),
        out_specs=P("exp", "seq"),
        check_vma=False,
    )
```

```python
import functools

import jax
import jax.numpy as jnp
import numpy as np
from jax import lax
from jax.experimental import pallas as pl
from jax.experimental.pallas import tpu as pltpu
from jax.sharding import PartitionSpec as P

BF = jnp.bfloat16
F32 = jnp.float32
MESH = pl.DeviceIdType.MESH
CHUNKS = 4
ORDERS = (("axb", "bxa"),) * 3 + (("abx", "bax"),)
OFFSETS = ((1, -1), (2, -2), (3, -3), (0, 4))


def dot(a, b):
    return jnp.dot(a, b, preferred_element_type=F32)


def dot_nt(a, b):
    return lax.dot_general(a, b, (((1,), (1,)), ((), ())), preferred_element_type=F32)


def dot_tn(a, b):
    return lax.dot_general(a, b, (((0,), (0,)), ((), ())), preferred_element_type=F32)


def cube_bit(d):
    s = lax.axis_index("seq")
    y, x = s // 2, s % 2
    return {"a": ((y + 1) // 2) % 2, "b": y // 2, "x": x}[d]


def cube_peer(d):
    s = lax.axis_index("seq")
    y, x = s // 2, s % 2
    there = {"a": (y + 1 - 2 * (y % 2)) * 2 + x, "b": (3 - y) * 2 + x, "x": y * 2 + 1 - x}[d]
    return (there, lax.axis_index("exp"))


def exp_peer(dz, dl, dc):
    e = lax.axis_index("exp")
    z, l, c = e // 4, (e // 2) % 2, e % 2
    return (((z + dz + 8) % 8) * 2 + (l + dl) % 2) * 2 + (c + dc) % 2


PLACES = tuple((m, dl, dc) for m in range(2) for dl in range(2) for dc in range(2))


def kernel(
    tok_ref, ids_ref, score_ref, cmat_ref, emat_ref, place_ref, back_ref, gate_ref, up_ref, down_ref, out_ref,
    place, back, wg, wu, wd, xs, code, wts, qw, snd, arr, rets, retr, part, r1, r2, r3, hid,
    w_sem, d_s, d_r, t_s, t_r, c_s, c_r,
):
    seq = lax.axis_index("seq")
    experts_dev, ff, _ = wg.shape
    half = ff // 2
    loads = [
        pltpu.make_async_copy(a, b, w_sem.at[i])
        for i, (a, b) in enumerate(
            ((place_ref, place), (gate_ref, wg), (up_ref, wu), (back_ref, back), (down_ref, wd))
        )
    ]
    for load in loads:
        load.start()

    barrier = pltpu.get_barrier_semaphore()
    for dz in range(8):
        for dl in range(2):
            for dc in range(2):
                if (dz, dl, dc) != (0, 0, 0):
                    pl.semaphore_signal(barrier, inc=1, device_id=(seq, exp_peer(dz, dl, dc)), device_id_type=MESH)
    for d in ("a", "b", "x"):
        pl.semaphore_signal(barrier, inc=1, device_id=cube_peer(d), device_id_type=MESH)

    topk, tok = ids_ref.shape
    expert = lax.broadcasted_iota(jnp.int32, code.shape, 0)
    row = lax.broadcasted_iota(jnp.int32, (tok, tok), 0)
    col = lax.broadcasted_iota(jnp.int32, (tok, tok), 1)
    scores = score_ref[...]
    weights = scores / jnp.sum(scores, axis=0, keepdims=True)
    named = jnp.zeros(code.shape, F32)
    dense = jnp.zeros(code.shape, F32)
    ids = ids_ref[...]
    for k in range(topk):
        hit = ids[k : k + 1] == expert
        named = named + jnp.where(hit, 1.0, 0.0)
        dense = dense + jnp.where(hit, weights[k : k + 1], 0.0)
    rank = dot(named.astype(BF), jnp.where(row < col, 1.0, 0.0).astype(BF))
    code[...] = jnp.where(named > 0.5, rank, -1.0)
    wts[...] = dense
    pl.semaphore_wait(barrier, 34)

    def dispatch(j, i):
        m, dl, dc = PLACES[i]
        slot = j * 8 + i
        return pltpu.make_async_remote_copy(
            src_ref=snd.at[slot], dst_ref=arr.at[slot], send_sem=d_s.at[slot], recv_sem=d_r.at[slot],
            device_id=(seq, exp_peer(-OFFSETS[j][m], dl, dc)), device_id_type=MESH,
        )

    def giveback(j, i):
        m, dl, dc = PLACES[i]
        slot = j * 8 + i
        return pltpu.make_async_remote_copy(
            src_ref=rets.at[slot], dst_ref=retr.at[slot], send_sem=t_s.at[slot], recv_sem=t_r.at[slot],
            device_id=(seq, exp_peer(OFFSETS[j][m], dl, dc)), device_id_type=MESH,
        )

    def is_self(j, i):
        return (OFFSETS[j][PLACES[i][0]], *PLACES[i][1:]) == (0, 0, 0)

    def both(ref, j, i):
        m, dl, dc = PLACES[i]
        d = exp_peer(-OFFSETS[j][m], dl, dc)
        first, second = (ref[pl.ds(2 * d + n, 1), :] for n in range(2))
        return jnp.where(
            emat_ref[...] > 0.5, jnp.concatenate([first, first], axis=1), jnp.concatenate([second, second], axis=1)
        )

    def slabs(j):
        chosen = [jnp.where(both(code, j, i) == cmat_ref[...], 1.0, 0.0).astype(BF) for i in range(8)]
        t2 = jnp.concatenate([tok_ref[:, :256], tok_ref[:, 256:]], axis=0)
        snd[pl.ds(j * 8, 8)] = dot(jnp.concatenate(chosen, axis=0), t2).astype(BF).reshape(8, 80, 256)
        for i in range(8):
            slot = j * 8 + i
            if is_self(j, i):
                pltpu.make_async_copy(snd.at[slot], arr.at[slot], d_r.at[slot]).start()
            else:
                dispatch(j, i).start()

    def weigh(j):
        for i in range(8):
            qw[j * 8 + i] = jnp.where(both(code, j, i) == cmat_ref[...], both(wts, j, i), 0.0).astype(BF)

    def copies(j, h):
        b1, b2, b3 = (cube_bit(d) for d in ORDERS[j][h])
        n1, n2, n3 = 1 - b1, 1 - b2, 1 - b3

        def at(p, q, r):
            return 4 * p + 2 * q + r

        own, third, second, last = at(b1, b2, b3), at(b1, b2, n3), at(b1, n2, b3), at(b1, n2, n3)
        return (
            (part, at(n1, n2, 0), 2, r1, 2 * n2, 0, 2 * n2),
            (part, at(n1, b2, 0), 2, r1, 2 * b2, 0, 2 * b2),
            (part, last, 1, r2, n3, 1, n3),
            (part, second, 1, r2, b3, 1, b3),
            (part, third, 1, r3, 0, 2, 0),
            (hid, own, 1, hid, own, 2, third),
            (hid, own, 1, hid, own, 1, second),
            (hid, third, 1, hid, third, 1, last),
            (hid, own, 1, hid, own, 0, at(n1, b2, b3)),
            (hid, third, 1, hid, third, 0, at(n1, b2, n3)),
            (hid, second, 1, hid, second, 0, at(n1, n2, b3)),
            (hid, last, 1, hid, last, 0, at(n1, n2, n3)),
        )

    def exchange(j, h, n):
        src, first, count, dst, there, along, _ = copies(j, h)[n]
        return pltpu.make_async_remote_copy(
            src_ref=src.at[j, h, pl.ds(first, count)], dst_ref=dst.at[j, h, pl.ds(there, count)],
            send_sem=c_s.at[j, h, n], recv_sem=c_r.at[j, h, n],
            device_id=cube_peer(ORDERS[j][h][along]), device_id_type=MESH,
        )

    def arrival(j, h, n):
        _, _, count, dst, _, _, first = copies(j, h)[n]
        ref = dst.at[j, h, pl.ds(first, count)]
        return pltpu.make_async_copy(ref, ref, c_r.at[j, h, n])

    def bits(j, h):
        return [cube_bit(d) for d in ORDERS[j][h]]

    def products(j):
        for i in range(8):
            slot = j * 8 + i
            pltpu.make_async_copy(arr.at[slot], arr.at[slot], d_r.at[slot]).wait()
        if j == 0:
            loads[0].wait()
        xs[...] = dot(place[...], arr[pl.ds(j * 8, 8)].reshape(640, 256)).astype(BF).reshape(4, 160, 256)
        if j == 0:
            loads[1].wait()
            loads[2].wait()
        for away in (1, 0):
            for h in range(2):
                b1 = bits(j, h)[0]
                e = 1 - b1 if away else b1
                g, u = (
                    dot_nt(xs[e], w[e, pl.ds(half * h, half), :256])
                    + dot_nt(xs[2 + e], w[e, pl.ds(half * h, half), 256:])
                    for w in (wg, wu)
                )
                for i in range(4):
                    part[j, h, 4 * e + i] = jnp.concatenate(
                        [g[40 * i : 40 * i + 40], u[40 * i : 40 * i + 40]], axis=0
                    ).astype(BF)
                if away:
                    exchange(j, h, 0).start()
                    exchange(j, h, 1).start()

    def sum1(j):
        for h in range(2):
            b1, b2, b3 = bits(j, h)
            arrival(j, h, 0).wait()
            for n, r in ((2, 1 - b3), (3, b3)):
                rel = 2 * (1 - b2) + r
                p = 4 * b1 + rel
                part[j, h, p] = (part[j, h, p].astype(F32) + r1[j, h, rel].astype(F32)).astype(BF)
                exchange(j, h, n).start()

    def sum2(j):
        for h in range(2):
            b1, b2, b3 = bits(j, h)
            arrival(j, h, 1).wait()
            arrival(j, h, 2).wait()
            rel = 2 * b2 + 1 - b3
            p = 4 * b1 + rel
            part[j, h, p] = (
                part[j, h, p].astype(F32) + r1[j, h, rel].astype(F32) + r2[j, h, 1 - b3].astype(F32)
            ).astype(BF)
            exchange(j, h, 4).start()

    def activate(j):
        for h in range(2):
            b1, b2, b3 = bits(j, h)
            arrival(j, h, 3).wait()
            arrival(j, h, 4).wait()
            rel = 2 * b2 + b3
            p = 4 * b1 + rel
            total = (
                part[j, h, p].astype(F32) + r1[j, h, rel].astype(F32)
                + r2[j, h, b3].astype(F32) + r3[j, h, 0].astype(F32)
            )
            g, u = total[:40], total[40:]
            v = g / (1.0 + jnp.exp(-g)) * u
            hid[j, h, p] = jnp.concatenate([v[:, :384], v[:, 384:]], axis=0).astype(BF)
            for n in (5, 6, 8):
                exchange(j, h, n).start()

    def pass_on(j, pairs):
        for n, after in pairs:
            for h in range(2):
                arrival(j, h, n).wait()
                for m in after:
                    exchange(j, h, m).start()

    def outputs(j):
        if j == 0:
            loads[3].wait()
            loads[4].wait()
        outs = [jnp.zeros((160, 512), F32) for _ in range(experts_dev)]
        for h in range(2):
            for n in (8, 9, 10, 11):
                arrival(j, h, n).wait()
            for e in range(experts_dev):
                pieces = [hid[j, h, 4 * e + i].astype(F32) for i in range(4)]
                block = jnp.concatenate([jnp.concatenate([v[:40], v[40:]], axis=1) for v in pieces], axis=0)
                outs[e] = outs[e] + dot(block.astype(BF), wd[e, pl.ds(half * h, half), :])
        tall = jnp.concatenate([o[:, n * 256 : n * 256 + 256] for n in range(2) for o in outs], axis=0).astype(BF)
        rets[pl.ds(j * 8, 8)] = dot(back[...], tall).astype(BF).reshape(8, 80, 256)
        for i in range(8):
            slot = j * 8 + i
            if is_self(j, i):
                pltpu.make_async_copy(rets.at[slot], retr.at[slot], t_r.at[slot]).start()
            else:
                giveback(j, i).start()

    stages = (
        products,
        sum1,
        sum2,
        activate,
        functools.partial(pass_on, pairs=((5, (7, 9)),)),
        functools.partial(pass_on, pairs=((6, (10,)), (7, (11,)))),
        outputs,
    )
    slabs(0)
    slabs(1)
    for t in range(CHUNKS + len(stages) - 1):
        for n in (0, 6, 5, 4, 3, 2, 1):
            if 0 <= t - n < CHUNKS:
                stages[n](t - n)
            if n == 0 and t == 0:
                slabs(2)
                slabs(3)
        if t < CHUNKS:
            weigh(t)

    total = jnp.zeros((256, 256), F32)
    for j in range(CHUNKS):
        for i in range(8):
            slot = j * 8 + i
            pltpu.make_async_copy(retr.at[slot], retr.at[slot], t_r.at[slot]).wait()
        total = total + dot_tn(qw[pl.ds(j * 8, 8)].reshape(640, 256), retr[pl.ds(j * 8, 8)].reshape(640, 256))
    out_ref[:, :256] = total[:tok].astype(BF)
    out_ref[:, 256:] = total[tok:].astype(BF)

    for j in range(CHUNKS):
        for i in range(8):
            if not is_self(j, i):
                dispatch(j, i).wait_send()
                giveback(j, i).wait_send()
        for h in range(2):
            for n in range(12):
                exchange(j, h, n).wait_send()


def placing(cap, blocks=8):
    n = 2 * 2 * blocks * cap
    out = np.zeros((n, n), np.float32)
    for b in range(blocks):
        for f in range(2):
            for e in range(2):
                for c in range(cap):
                    out[((f * 2 + e) * blocks + b) * cap + c, ((b * 2 + f) * 2 + e) * cap + c] = 1.0
    return out


def per_device(tokens, expert_ids, gate_scores, gate_proj, up_proj, down_proj):
    cap = 20
    place = placing(cap)
    r = np.arange(4 * cap)[:, None]
    t = np.arange(256)[None, :]
    cmat = np.where(r // (2 * cap) == t // 128, r % cap, -9).astype(np.float32)
    emat = np.broadcast_to((r // cap) % 2 == 0, cmat.shape).astype(np.float32)
    vmem = pl.BlockSpec(memory_space=pltpu.VMEM)
    hbm = pl.BlockSpec(memory_space=pl.ANY)
    dma = pltpu.SemaphoreType.DMA
    weights = pltpu.VMEM(gate_proj.shape, BF)
    slabs = pltpu.VMEM((32, 80, 256), BF)
    return pl.pallas_call(
        kernel,
        out_shape=jax.ShapeDtypeStruct(tokens.shape, BF),
        in_specs=[vmem] * 5 + [hbm] * 5,
        out_specs=vmem,
        scratch_shapes=[
            pltpu.VMEM(place.shape, BF), pltpu.VMEM(place.shape, BF),
            weights, weights, weights, pltpu.VMEM((4, 160, 256), BF),
            pltpu.VMEM((64, 128), F32), pltpu.VMEM((64, 128), F32),
            slabs, slabs, slabs, slabs, slabs,
            pltpu.VMEM((CHUNKS, 2, 8, 80, 768), BF),
            pltpu.VMEM((CHUNKS, 2, 4, 80, 768), BF),
            pltpu.VMEM((CHUNKS, 2, 2, 80, 768), BF),
            pltpu.VMEM((CHUNKS, 2, 1, 80, 768), BF),
            pltpu.VMEM((CHUNKS, 2, 8, 80, 384), BF),
            dma((5,)), dma((32,)), dma((32,)), dma((32,)), dma((32,)), dma((CHUNKS, 2, 12)), dma((CHUNKS, 2, 12)),
        ],
        compiler_params=pltpu.CompilerParams(
            collective_id=0, has_side_effects=True, vmem_limit_bytes=60 * 2**20
        ),
        name="experts",
    )(
        tokens, expert_ids.T, gate_scores.T, jnp.asarray(cmat), jnp.asarray(emat),
        jnp.asarray(place, BF), jnp.asarray(place.T, BF), gate_proj, up_proj, down_proj,
    )


def solution(mesh):
    return jax.shard_map(
        per_device,
        mesh=mesh,
        in_specs=(
            P("exp", "seq"),
            P("exp", None),
            P("exp", None),
            P("exp", None, "seq"),
            P("exp", None, "seq"),
            P("exp", None, "seq"),
        ),
        out_specs=P("exp", "seq"),
        check_vma=False,
    )
```

```python
import functools

import jax
import jax.numpy as jnp
import numpy as np
from jax import lax
from jax.experimental import pallas as pl
from jax.experimental.pallas import tpu as pltpu
from jax.sharding import PartitionSpec as P

BF = jnp.bfloat16
F32 = jnp.float32
MESH = pl.DeviceIdType.MESH
CHUNKS = 4
ORDERS = (("axb", "bxa"),) * 3 + (("abx", "bax"),)
OFFSETS = ((1, -1), (3, -3), (2, -2), (0, 4))


def dot(a, b):
    return jnp.dot(a, b, preferred_element_type=F32)


def dot_nt(a, b):
    return lax.dot_general(a, b, (((1,), (1,)), ((), ())), preferred_element_type=F32)


def cube_bit(d):
    s = lax.axis_index("seq")
    y, x = s // 2, s % 2
    return {"a": ((y + 1) // 2) % 2, "b": y // 2, "x": x}[d]


def cube_peer(d):
    s = lax.axis_index("seq")
    y, x = s // 2, s % 2
    there = {"a": (y + 1 - 2 * (y % 2)) * 2 + x, "b": (3 - y) * 2 + x, "x": y * 2 + 1 - x}[d]
    return (there, lax.axis_index("exp"))


def exp_peer(dz, dl, dc):
    e = lax.axis_index("exp")
    z, l, c = e // 4, (e // 2) % 2, e % 2
    return (((z + dz + 8) % 8) * 2 + (l + dl) % 2) * 2 + (c + dc) % 2


PLACES = tuple((m, dl, dc) for m in range(2) for dl in range(2) for dc in range(2))


def kernel(
    tok_ref, ids_ref, score_ref, cmat_ref, emat_ref, place_ref, back_ref, gate_ref, up_ref, down_ref, out_ref,
    place, back, wg, wu, wd, xs, code, wts, qw, snd, arr, rets, retr, part, r1, r2, r3, hid,
    w_sem, d_s, d_r, t_s, t_r, c_s, c_r,
):
    seq = lax.axis_index("seq")
    experts_dev, ff, _ = wg.shape
    half = ff // 2
    loads = [
        pltpu.make_async_copy(a, b, w_sem.at[i])
        for i, (a, b) in enumerate(
            ((place_ref, place), (gate_ref, wg), (up_ref, wu), (back_ref, back), (down_ref, wd))
        )
    ]
    for load in loads:
        load.start()

    barrier = pltpu.get_barrier_semaphore()
    for dz in range(8):
        for dl in range(2):
            for dc in range(2):
                if (dz, dl, dc) != (0, 0, 0):
                    pl.semaphore_signal(barrier, inc=1, device_id=(seq, exp_peer(dz, dl, dc)), device_id_type=MESH)
    for d in ("a", "b", "x"):
        pl.semaphore_signal(barrier, inc=1, device_id=cube_peer(d), device_id_type=MESH)

    topk, tok = ids_ref.shape
    expert = lax.broadcasted_iota(jnp.int32, code.shape, 0)
    row = lax.broadcasted_iota(jnp.int32, (tok, tok), 0)
    col = lax.broadcasted_iota(jnp.int32, (tok, tok), 1)
    scores = score_ref[...]
    weights = scores / jnp.sum(scores, axis=0, keepdims=True)
    named = jnp.zeros(code.shape, F32)
    dense = jnp.zeros(code.shape, F32)
    ids = ids_ref[...]
    for k in range(topk):
        hit = ids[k : k + 1] == expert
        named = named + jnp.where(hit, 1.0, 0.0)
        dense = dense + jnp.where(hit, weights[k : k + 1], 0.0)
    rank = dot(named.astype(BF), jnp.where(row < col, 1.0, 0.0).astype(BF))
    code[...] = jnp.where(named > 0.5, rank, -1.0)
    wts[...] = dense
    pl.semaphore_wait(barrier, 34)

    def dispatch(j, i):
        m, dl, dc = PLACES[i]
        slot = j * 8 + i
        return pltpu.make_async_remote_copy(
            src_ref=snd.at[slot], dst_ref=arr.at[slot], send_sem=d_s.at[slot], recv_sem=d_r.at[slot],
            device_id=(seq, exp_peer(-OFFSETS[j][m], dl, dc)), device_id_type=MESH,
        )

    def giveback(j, i):
        m, dl, dc = PLACES[i]
        slot = j * 8 + i
        return pltpu.make_async_remote_copy(
            src_ref=rets.at[slot], dst_ref=retr.at[slot], send_sem=t_s.at[slot], recv_sem=t_r.at[slot],
            device_id=(seq, exp_peer(OFFSETS[j][m], dl, dc)), device_id_type=MESH,
        )

    def is_self(j, i):
        return (OFFSETS[j][PLACES[i][0]], *PLACES[i][1:]) == (0, 0, 0)

    def both(ref, j, i):
        m, dl, dc = PLACES[i]
        d = exp_peer(-OFFSETS[j][m], dl, dc)
        first, second = (ref[pl.ds(2 * d + n, 1), :] for n in range(2))
        return jnp.where(
            emat_ref[...] > 0.5, jnp.concatenate([first, first], axis=1), jnp.concatenate([second, second], axis=1)
        )

    def slabs(j):
        chosen = [jnp.where(both(code, j, i) == cmat_ref[...], 1.0, 0.0).astype(BF) for i in range(8)]
        t2 = jnp.concatenate([tok_ref[:, :256], tok_ref[:, 256:]], axis=0)
        snd[pl.ds(j * 8, 8)] = dot(jnp.concatenate(chosen, axis=0), t2).astype(BF).reshape(8, 80, 256)
        for i in range(8):
            slot = j * 8 + i
            if is_self(j, i):
                pltpu.make_async_copy(snd.at[slot], arr.at[slot], d_r.at[slot]).start()
            else:
                dispatch(j, i).start()

    def weigh(j):
        shares = [jnp.where(both(code, j, i) == cmat_ref[...], both(wts, j, i), 0.0) for i in range(8)]
        qw[j] = jnp.concatenate(shares, axis=0).T.astype(BF)

    def copies(j, h):
        b1, b2, b3 = (cube_bit(d) for d in ORDERS[j][h])
        n1, n2, n3 = 1 - b1, 1 - b2, 1 - b3

        def at(p, q, r):
            return 4 * p + 2 * q + r

        own, third, second, last = at(b1, b2, b3), at(b1, b2, n3), at(b1, n2, b3), at(b1, n2, n3)
        return (
            (part, at(n1, n2, 0), 2, r1, 2 * n2, 0, 2 * n2),
            (part, at(n1, b2, 0), 2, r1, 2 * b2, 0, 2 * b2),
            (part, last, 1, r2, n3, 1, n3),
            (part, second, 1, r2, b3, 1, b3),
            (part, third, 1, r3, 0, 2, 0),
            (hid, own, 1, hid, own, 2, third),
            (hid, own, 1, hid, own, 1, second),
            (hid, third, 1, hid, third, 1, last),
            (hid, own, 1, hid, own, 0, at(n1, b2, b3)),
            (hid, third, 1, hid, third, 0, at(n1, b2, n3)),
            (hid, second, 1, hid, second, 0, at(n1, n2, b3)),
            (hid, last, 1, hid, last, 0, at(n1, n2, n3)),
        )

    def exchange(j, h, n):
        src, first, count, dst, there, along, _ = copies(j, h)[n]
        return pltpu.make_async_remote_copy(
            src_ref=src.at[j, h, pl.ds(first, count)], dst_ref=dst.at[j, h, pl.ds(there, count)],
            send_sem=c_s.at[j, h, n], recv_sem=c_r.at[j, h, n],
            device_id=cube_peer(ORDERS[j][h][along]), device_id_type=MESH,
        )

    def arrival(j, h, n):
        _, _, count, dst, _, _, first = copies(j, h)[n]
        ref = dst.at[j, h, pl.ds(first, count)]
        return pltpu.make_async_copy(ref, ref, c_r.at[j, h, n])

    def bits(j, h):
        return [cube_bit(d) for d in ORDERS[j][h]]

    def products(j):
        for i in range(8):
            slot = j * 8 + i
            pltpu.make_async_copy(arr.at[slot], arr.at[slot], d_r.at[slot]).wait()
        if j == 0:
            loads[0].wait()
        xs[...] = dot(place[...], arr[pl.ds(j * 8, 8)].reshape(640, 256)).astype(BF).reshape(4, 160, 256)
        if j == 0:
            loads[1].wait()
            loads[2].wait()
        for away in (1, 0):
            for h in range(2):
                b1 = bits(j, h)[0]
                e = 1 - b1 if away else b1
                g, u = (
                    dot_nt(xs[e], w[e, pl.ds(half * h, half), :256])
                    + dot_nt(xs[2 + e], w[e, pl.ds(half * h, half), 256:])
                    for w in (wg, wu)
                )
                for i in range(4):
                    part[j, h, 4 * e + i] = jnp.concatenate(
                        [g[40 * i : 40 * i + 40], u[40 * i : 40 * i + 40]], axis=0
                    ).astype(BF)
                if away:
                    exchange(j, h, 0).start()
                    exchange(j, h, 1).start()

    def sum1(j):
        for h in range(2):
            b1, b2, b3 = bits(j, h)
            arrival(j, h, 0).wait()
            for n, r in ((2, 1 - b3), (3, b3)):
                rel = 2 * (1 - b2) + r
                p = 4 * b1 + rel
                part[j, h, p] = (part[j, h, p].astype(F32) + r1[j, h, rel].astype(F32)).astype(BF)
                exchange(j, h, n).start()

    def sum2(j):
        for h in range(2):
            b1, b2, b3 = bits(j, h)
            arrival(j, h, 1).wait()
            arrival(j, h, 2).wait()
            rel = 2 * b2 + 1 - b3
            p = 4 * b1 + rel
            part[j, h, p] = (
                part[j, h, p].astype(F32) + r1[j, h, rel].astype(F32) + r2[j, h, 1 - b3].astype(F32)
            ).astype(BF)
            exchange(j, h, 4).start()

    def activate(j):
        for h in range(2):
            b1, b2, b3 = bits(j, h)
            arrival(j, h, 3).wait()
            arrival(j, h, 4).wait()
            rel = 2 * b2 + b3
            p = 4 * b1 + rel
            total = (
                part[j, h, p].astype(F32) + r1[j, h, rel].astype(F32)
                + r2[j, h, b3].astype(F32) + r3[j, h, 0].astype(F32)
            )
            g, u = total[:40], total[40:]
            v = g / (1.0 + jnp.exp(-g)) * u
            hid[j, h, p] = jnp.concatenate([v[:, :384], v[:, 384:]], axis=0).astype(BF)
            for n in (5, 6, 8):
                exchange(j, h, n).start()

    def pass_on(j, pairs):
        for n, after in pairs:
            for h in range(2):
                arrival(j, h, n).wait()
                for m in after:
                    exchange(j, h, m).start()

    def outputs(j):
        if j == 0:
            loads[3].wait()
            loads[4].wait()
        outs = [jnp.zeros((160, 512), F32) for _ in range(experts_dev)]
        for h in range(2):
            for n in (8, 9, 10, 11):
                arrival(j, h, n).wait()
            for e in range(experts_dev):
                pieces = [hid[j, h, 4 * e + i].astype(F32) for i in range(4)]
                block = jnp.concatenate([jnp.concatenate([v[:40], v[40:]], axis=1) for v in pieces], axis=0)
                outs[e] = outs[e] + dot(block.astype(BF), wd[e, pl.ds(half * h, half), :])
        tall = jnp.concatenate([o[:, n * 256 : n * 256 + 256] for n in range(2) for o in outs], axis=0).astype(BF)
        rets[pl.ds(j * 8, 8)] = dot(back[...], tall).astype(BF).reshape(8, 80, 256)
        for i in range(8):
            slot = j * 8 + i
            if is_self(j, i):
                pltpu.make_async_copy(rets.at[slot], retr.at[slot], t_r.at[slot]).start()
            else:
                giveback(j, i).start()

    stages = (
        products,
        sum1,
        sum2,
        activate,
        functools.partial(pass_on, pairs=((5, (7, 9)),)),
        functools.partial(pass_on, pairs=((6, (10,)), (7, (11,)))),
        outputs,
    )
    slabs(0)
    slabs(1)
    for t in range(CHUNKS + len(stages) - 1):
        for n in (0, 6, 5, 4, 3, 2, 1):
            if 0 <= t - n < CHUNKS:
                stages[n](t - n)
            if n == 0 and t == 0:
                slabs(2)
                slabs(3)
        if t == 0:
            for j in range(CHUNKS):
                weigh(j)

    total = jnp.zeros((256, 256), F32)
    for j in range(CHUNKS):
        for i in range(8):
            slot = j * 8 + i
            pltpu.make_async_copy(retr.at[slot], retr.at[slot], t_r.at[slot]).wait()
        total = total + dot(qw[j], retr[pl.ds(j * 8, 8)].reshape(640, 256))
    out_ref[:, :256] = total[:tok].astype(BF)
    out_ref[:, 256:] = total[tok:].astype(BF)

    for j in range(CHUNKS):
        for i in range(8):
            if not is_self(j, i):
                dispatch(j, i).wait_send()
                giveback(j, i).wait_send()
        for h in range(2):
            for n in range(12):
                exchange(j, h, n).wait_send()


def placing(cap, blocks=8):
    n = 2 * 2 * blocks * cap
    out = np.zeros((n, n), np.float32)
    for b in range(blocks):
        for f in range(2):
            for e in range(2):
                for c in range(cap):
                    out[((f * 2 + e) * blocks + b) * cap + c, ((b * 2 + f) * 2 + e) * cap + c] = 1.0
    return out


def per_device(tokens, expert_ids, gate_scores, gate_proj, up_proj, down_proj):
    cap = 20
    place = placing(cap)
    r = np.arange(4 * cap)[:, None]
    t = np.arange(256)[None, :]
    cmat = np.where(r // (2 * cap) == t // 128, r % cap, -9).astype(np.float32)
    emat = np.broadcast_to((r // cap) % 2 == 0, cmat.shape).astype(np.float32)
    vmem = pl.BlockSpec(memory_space=pltpu.VMEM)
    hbm = pl.BlockSpec(memory_space=pl.ANY)
    dma = pltpu.SemaphoreType.DMA
    weights = pltpu.VMEM(gate_proj.shape, BF)
    slabs = pltpu.VMEM((32, 80, 256), BF)
    return pl.pallas_call(
        kernel,
        out_shape=jax.ShapeDtypeStruct(tokens.shape, BF),
        in_specs=[vmem] * 5 + [hbm] * 5,
        out_specs=vmem,
        scratch_shapes=[
            pltpu.VMEM(place.shape, BF), pltpu.VMEM(place.shape, BF),
            weights, weights, weights, pltpu.VMEM((4, 160, 256), BF),
            pltpu.VMEM((64, 128), F32), pltpu.VMEM((64, 128), F32),
            pltpu.VMEM((CHUNKS, 256, 640), BF), slabs, slabs, slabs, slabs,
            pltpu.VMEM((CHUNKS, 2, 8, 80, 768), BF),
            pltpu.VMEM((CHUNKS, 2, 4, 80, 768), BF),
            pltpu.VMEM((CHUNKS, 2, 2, 80, 768), BF),
            pltpu.VMEM((CHUNKS, 2, 1, 80, 768), BF),
            pltpu.VMEM((CHUNKS, 2, 8, 80, 384), BF),
            dma((5,)), dma((32,)), dma((32,)), dma((32,)), dma((32,)), dma((CHUNKS, 2, 12)), dma((CHUNKS, 2, 12)),
        ],
        compiler_params=pltpu.CompilerParams(
            collective_id=0, has_side_effects=True, vmem_limit_bytes=60 * 2**20
        ),
        name="experts",
    )(
        tokens, expert_ids.T, gate_scores.T, jnp.asarray(cmat), jnp.asarray(emat),
        jnp.asarray(place, BF), jnp.asarray(place.T, BF), gate_proj, up_proj, down_proj,
    )


def solution(mesh):
    return jax.shard_map(
        per_device,
        mesh=mesh,
        in_specs=(
            P("exp", "seq"),
            P("exp", None),
            P("exp", None),
            P("exp", None, "seq"),
            P("exp", None, "seq"),
            P("exp", None, "seq"),
        ),
        out_specs=P("exp", "seq"),
        check_vma=False,
    )
```
